32 devices in a mesh: dp: 8 (over z, y), tensor: 4 (over x, core).
Axes of the slice: x: 2, y: 2, z: 4, core: 2. Of those that a mesh axis runs over, the one named last changes fastest.
Arguments:
- query: bfloat16 [16, 128, 8192], P('dp', None, 'tensor'), may hold values from -6 to 6
- image: bfloat16 [16, 512, 8192], P('dp', None, 'tensor'), may hold values from -6 to 6
- tiles: int32 [16], replicated, may hold values from 0 to 4, as said below
- image_slot: int32 [16], replicated, may hold values from 0 to 15, as said below
- key_weight_matrix: bfloat16 [8192, 1024], P('dp', 'tensor'), may hold values from -0.0625 to 0.0625
- value_weight_matrix: bfloat16 [8192, 1024], P('dp', 'tensor'), may hold values from -0.0625 to 0.0625
- query_gain: float32 [128], replicated, may hold values from 0.5 to 2
- key_gain: float32 [128], replicated, may hold values from 0.5 to 2
- gate: float32 [1], replicated, may hold values from 0.3 to 1.5
- cotangent: bfloat16 [16, 128, 8192], P('dp', None, 'tensor'), may hold values from -6 to 6
Outputs:
- context: bfloat16 [16, 128, 8192], P('dp', None, 'tensor')
- d_query: bfloat16 [16, 128, 8192], P('dp', None, 'tensor')
- d_w_key: float32 [8192, 1024], P('dp', 'tensor')
- d_w_value: float32 [8192, 1024], P('dp', 'tensor')
The draws below stay inside these ranges and needn't reach their ends.
Inputs may be any that keep to these rules, and one draw needn't show every extreme that they name: Some sample has 4 tiles and some has none. image_slot is a permutation of the samples. Sample s sits at dp index s // 2; the image rows image_slot[s] sit at the same dp index or at the one that differs from it by half the dp axis, and of the two samples at one dp index at most one has its image at the other index.
All inputs are finite; a program needn't handle non-finite values.
Results may differ from the reference program's by a relative error of at most 0.02.
Values may be sent and summed in bfloat16 or wider, within the bound.
A program may use at most 192 MiB of HBM per device.

```python
import math
import jax
import jax.numpy as jnp
from jax import lax

MODEL_WIDTH = 8192
HQ = 64
KEY_VALUE_HEADS = 8
HEAD_SIZE = 128
TXT = 128
TILE = 128
MAX_TILES = 4
IMG = 512
SAMPLES = 16
N_DP = 8


def tile_counts(key):
    counts = jax.random.randint(jax.random.fold_in(key, 11), (SAMPLES,), 0, MAX_TILES + 1)
    order = jax.random.permutation(jax.random.fold_in(key, 12), SAMPLES)
    counts = counts.at[order[0]].set(MAX_TILES)
    counts = counts.at[order[1]].set(0)
    return counts.astype(jnp.int32)


def draw_tiles(key, part):
    return tile_counts(key)


def draw_image_slot(key, part):
    counts = tile_counts(key)
    half = N_DP // 2
    shard = jnp.arange(half, dtype=jnp.int32)
    first = 2 * shard
    second = first + 1
    third = 2 * (shard + half)
    fourth = third + 1
    load_a = counts[first]
    load_b = counts[second]
    load_c = counts[third]
    load_d = counts[fourth]
    loads = jnp.stack([jnp.maximum(load_a + load_c, load_b + load_d), jnp.maximum(load_a + load_d, load_b + load_c), jnp.maximum(load_a + load_b, load_c + load_d)])
    best = jnp.argmin(loads, axis=0).astype(jnp.int32)
    slot_b = jnp.where(best == 2, second, third)
    slot_c = jnp.where(best == 0, second, jnp.where(best == 1, fourth, third))
    slot_d = jnp.where(best == 1, second, fourth)
    slots = jnp.zeros((SAMPLES,), jnp.int32)
    slots = slots.at[first].set(first).at[second].set(slot_b)
    slots = slots.at[third].set(slot_c).at[fourth].set(slot_d)
    return slots.astype(jnp.int32)


def strengthened(values, own_key, source, target, blocks, factor):
    def block_of(dim):
        return (jnp.arange(values.shape[dim]) // (values.shape[dim] // blocks)).reshape((-1,) + (1,) * (values.ndim - 1 - dim))

    first = jax.random.permutation(own_key, blocks)[block_of(target)]
    second = (block_of(target) + blocks // 2) % blocks
    return jnp.where((block_of(source) == first) | (block_of(source) == second), factor * values, values)


def levels(key, extent, cuts, low, high):
    factor_of = 1.0
    for position, parts in cuts:
        steps = jax.random.uniform(jax.random.fold_in(jax.random.fold_in(key, 6), position), (parts,), jnp.float32, low / len(cuts), high / len(cuts))
        factor_of = factor_of * jnp.repeat(jnp.exp(steps), extent[position] // parts).reshape((-1,) + (1,) * (len(extent) - 1 - position))
    return factor_of


def noise(stream_key, shape, spread, bound, pieces=(), held_as=jnp.bfloat16):
    entries = spread * jax.random.normal(stream_key, shape, jnp.float32)
    if pieces:
        entries = entries * levels(stream_key, shape, pieces, -0.22, 0.18)
    return jnp.clip(entries, -bound, bound).astype(held_as)


def heavy_noise(own_key, shape, spread, limit, cuts, heavy, kind=jnp.bfloat16):
    drawn = spread * jax.random.normal(own_key, shape, jnp.float32)
    if cuts:
        drawn = drawn * levels(own_key, shape, cuts, -0.22, 0.18)
    return jnp.clip(strengthened(drawn, jax.random.fold_in(own_key, 3), *heavy), -limit, limit).astype(kind)


def setup_inputs(seed: int = 0) -> dict:
    key_list = jax.random.split(jax.random.key(seed), 11)
    return {
        "query": noise(key_list[0], (SAMPLES, TXT, HQ * HEAD_SIZE), 1.0, 6.0, ((0, 8), (2, 4))),
        "image": heavy_noise(key_list[1], (SAMPLES, IMG, MODEL_WIDTH), 1.0, 6.0, ((0, 8), (2, 4)), (0, 2, 8, 2.0)),
        "tiles": draw_tiles(jax.random.fold_in(key_list[10], 71), 0),
        "image_slot": draw_image_slot(jax.random.fold_in(key_list[10], 71), 0),
        "key_weight_matrix": noise(key_list[4], (MODEL_WIDTH, KEY_VALUE_HEADS * HEAD_SIZE), MODEL_WIDTH ** -0.5, 0.0625, ((0, 8), (1, 4))),
        "value_weight_matrix": noise(key_list[5], (MODEL_WIDTH, KEY_VALUE_HEADS * HEAD_SIZE), MODEL_WIDTH ** -0.5, 0.0625, ((0, 8), (1, 4))),
        "query_gain": jnp.clip(jnp.exp(jax.random.uniform(key_list[6], (HEAD_SIZE,), jnp.float32, math.log(0.5), math.log(2.0))), 0.5, 2.0),
        "key_gain": jnp.clip(jnp.exp(jax.random.uniform(key_list[7], (HEAD_SIZE,), jnp.float32, math.log(0.5), math.log(2.0))), 0.5, 2.0),
        "gate": jnp.clip(jax.random.uniform(key_list[8], (1,), jnp.float32, 0.3, 1.5), 0.3, 1.5),
        "cotangent": noise(key_list[9], (SAMPLES, TXT, HQ * HEAD_SIZE), 1.0, 6.0, ((0, 8), (2, 4))),
    }


EPS = 1e-06

def rms_factor(values):
    return lax.rsqrt(lax.optimization_barrier(jnp.mean(values * values, axis=-1, keepdims=True)) + EPS)

def norm_back(values, norm_multiplier, gain, grad):
    weighted = grad * gain
    inner = lax.optimization_barrier(jnp.sum(weighted * values, axis=-1, keepdims=True))
    return norm_multiplier * weighted - values * (norm_multiplier * norm_multiplier * norm_multiplier) * inner / values.shape[-1]

def reference(query, image, tiles, image_slot, key_weight_matrix, value_weight_matrix, query_gain, key_gain, gate, cotangent):
    head_dim = query_gain.shape[0]
    kv_cols = key_weight_matrix.shape[1]
    kv_heads = kv_cols // head_dim
    group = query.shape[2] // kv_cols
    text_rows = query.shape[1]
    img_rows = image.shape[1]
    ratio = jnp.tanh(gate[0])
    scale = head_dim ** (-0.5)
    key_pos = jnp.arange(img_rows, dtype=jnp.int32)

    def one_sample(carry, inputs):
        q_in, cot_in, count, slot = inputs
        feats = lax.dynamic_index_in_dim(image, slot.astype(jnp.int32), 0, keepdims=False)
        kraw = jnp.dot(feats, key_weight_matrix, preferred_element_type=jnp.float32).reshape(img_rows, kv_heads, head_dim)
        vals = jnp.dot(feats, value_weight_matrix, preferred_element_type=jnp.float32).astype(jnp.bfloat16)
        vals = vals.reshape(img_rows, kv_heads, head_dim)
        key_factor = rms_factor(kraw)
        keys = (kraw * key_factor * key_gain).astype(jnp.bfloat16)
        q_raw = q_in.astype(jnp.float32).reshape(text_rows, kv_heads, group, head_dim)
        q_factor = rms_factor(q_raw)
        q_norm = (q_raw * q_factor * query_gain).astype(jnp.bfloat16)
        scores = jnp.einsum('tkgd,skd->kgts', q_norm.astype(jnp.float32), keys.astype(jnp.float32)) * scale
        valid = key_pos < count * TILE
        expo = jnp.where(valid, jnp.exp(scores), 0.0)
        total = lax.optimization_barrier(jnp.sum(expo, axis=-1, keepdims=True)) + (count == 0).astype(jnp.float32)
        total_rows = jnp.transpose(total[..., 0], (2, 0, 1))[..., None]
        weights_b = expo.astype(jnp.bfloat16)
        attended = jnp.einsum('kgts,skd->tkgd', weights_b.astype(jnp.float32), vals.astype(jnp.float32)) / total_rows
        context = (ratio * attended).astype(jnp.bfloat16).reshape(text_rows, -1)
        d_att = ratio * cot_in.astype(jnp.float32).reshape(text_rows, kv_heads, group, head_dim)
        d_att_b = d_att.astype(jnp.bfloat16)
        scaled_b = (d_att / total_rows).astype(jnp.bfloat16)
        delta = jnp.transpose(lax.optimization_barrier(jnp.sum(d_att * attended, axis=-1)), (1, 2, 0))[..., None]
        d_prob = jnp.einsum('tkgd,skd->kgts', d_att_b.astype(jnp.float32), vals.astype(jnp.float32))
        d_score = (expo / total * (d_prob - delta)).astype(jnp.bfloat16).astype(jnp.float32)
        d_qn = scale * jnp.einsum('kgts,skd->tkgd', d_score, keys.astype(jnp.float32))
        d_query = norm_back(q_raw, q_factor, query_gain, d_qn).astype(jnp.bfloat16).reshape(text_rows, -1)
        d_keys = scale * jnp.einsum('kgts,tkgd->skd', d_score, q_norm.astype(jnp.float32))
        d_vals = jnp.einsum('kgts,tkgd->skd', weights_b.astype(jnp.float32), scaled_b.astype(jnp.float32))
        grad_key_unnormed = norm_back(kraw, key_factor, key_gain, d_keys).astype(jnp.bfloat16).reshape(img_rows, -1)
        d_vals_b = d_vals.astype(jnp.bfloat16).reshape(img_rows, -1)
        dims = (((0,), (0,)), ((), ()))
        grad_key = lax.dot_general(feats, grad_key_unnormed, dims, preferred_element_type=jnp.float32)
        grad_value = lax.dot_general(feats, d_vals_b, dims, preferred_element_type=jnp.float32)
        return ((carry[0] + grad_key, carry[1] + grad_value), (context, d_query))
    start = (jnp.zeros(key_weight_matrix.shape, jnp.float32), jnp.zeros(value_weight_matrix.shape, jnp.float32))
    grads, outputs = lax.scan(one_sample, start, (query, cotangent, tiles, image_slot))
    return (outputs[0], outputs[1], grads[0], grads[1])
```

```python
import functools

import jax
import jax.numpy as jnp
from jax import lax
from jax.experimental import pallas as pl
from jax.experimental.pallas import tpu as pltpu
from jax.sharding import PartitionSpec as P

TILE = 128


EPS = 1e-06


def swapped(shard, axis, distance):
    return lax.ppermute(shard, axis, [(i, i ^ 1 << distance) for i in range(lax.axis_size(axis))])


def rms_factor(values):
    return lax.rsqrt(jnp.mean(values * values, axis=-1, keepdims=True) + EPS)


def norm_back(values, norm_multiplier, gain, grad):
    weighted = grad * gain
    inner = jnp.sum(weighted * values, axis=-1, keepdims=True)
    return (
        norm_multiplier * weighted
        - values * (norm_multiplier * norm_multiplier * norm_multiplier) * inner / values.shape[-1]
    )


def attend_kernel(
    group, source, count, q_ref, cot_ref, kv_ref, gain_ref, ratio_ref, ctx_ref, dq_ref, dkv_ref
):
    own = pl.program_id(0)
    rows = kv_ref.shape[1]
    dim = kv_ref.shape[2] // 2
    text = q_ref.shape[1]
    scale = dim ** (-0.5)
    f32 = jnp.float32
    bf16 = jnp.bfloat16
    tiles = count[own]
    ratio = ratio_ref[0]
    empty = (tiles == 0).astype(f32)
    gain = gain_ref[...]
    keys = kv_ref[0, :, :dim]
    vals = kv_ref[0, :, dim:]
    keys_t = keys.T
    vals_t = vals.T
    at_once = 2 if group % 2 == 0 else 1
    valid = lax.broadcasted_iota(jnp.int32, (rows, at_once * text), 0) < tiles * TILE
    across = (((1,), (1,)), ((), ()))
    d_keys = jnp.zeros((rows, dim), f32)
    d_vals = jnp.zeros((rows, dim), f32)

    def load(ref, first):
        parts = [
            ref[0, :, (first + i) * dim : (first + i + 1) * dim].astype(f32).T
            for i in range(at_once)
        ]
        return jnp.concatenate(parts, axis=1)

    def store(ref, first, value):
        for i in range(at_once):
            part = value[:, i * text : (i + 1) * text].T
            ref[0, :, (first + i) * dim : (first + i + 1) * dim] = part.astype(bf16)

    for first in range(0, group, at_once):
        q_raw = load(q_ref, first)
        d_att = ratio * load(cot_ref, first)
        q_factor = lax.rsqrt(jnp.mean(q_raw * q_raw, axis=0, keepdims=True) + EPS)
        q_norm = (q_raw * q_factor * gain).astype(bf16)
        scores = jnp.dot(keys, q_norm, preferred_element_type=f32) * scale
        expo = jnp.where(valid, jnp.exp(scores), 0.0)
        total = jnp.sum(expo, axis=0, keepdims=True) + empty
        inverse = 1.0 / total
        weights_b = expo.astype(bf16)
        attended = jnp.dot(vals_t, weights_b, preferred_element_type=f32) * inverse
        store(ctx_ref, first, ratio * attended)
        d_att_b = d_att.astype(bf16)
        scaled_b = (d_att * inverse).astype(bf16)
        delta = jnp.sum(d_att * attended, axis=0, keepdims=True)
        d_prob = jnp.dot(vals, d_att_b, preferred_element_type=f32)
        d_score = (expo * inverse * (d_prob - delta)).astype(bf16)
        d_qn = scale * jnp.dot(keys_t, d_score, preferred_element_type=f32)
        weighted = d_qn * gain
        inner = jnp.sum(weighted * q_raw, axis=0, keepdims=True)
        cubed = q_factor * q_factor * q_factor
        store(dq_ref, first, q_factor * weighted - q_raw * (cubed * inner / dim))
        d_keys += lax.dot_general(d_score, q_norm, across, preferred_element_type=f32)
        d_vals += lax.dot_general(weights_b, scaled_b, across, preferred_element_type=f32)
    dkv_ref[0, :, :dim] = (scale * d_keys).astype(bf16)
    dkv_ref[0, :, dim:] = d_vals.astype(bf16)


def attend(query, cot, kv, source, count, gain, ratio, kv_local, head_dim):
    samples, text, cols = query.shape
    img_rows = kv.shape[1]
    group = cols // (kv_local * head_dim)
    per_head = pl.BlockSpec((1, text, group * head_dim), lambda s, k, *_: (s, 0, k))
    flops = 12 * samples * text * cols * img_rows
    return pl.pallas_call(
        functools.partial(attend_kernel, group),
        grid_spec=pltpu.PrefetchScalarGridSpec(
            num_scalar_prefetch=2,
            grid=(samples, kv_local),
            in_specs=[
                per_head,
                per_head,
                pl.BlockSpec(
                    (1, img_rows, 2 * head_dim), lambda s, k, source, count: (source[s], 0, k)
                ),
                pl.BlockSpec((head_dim, 1), lambda s, k, *_: (0, 0)),
                pl.BlockSpec(memory_space=pltpu.SMEM),
            ],
            out_specs=[
                per_head,
                per_head,
                pl.BlockSpec((1, img_rows, 2 * head_dim), lambda s, k, *_: (s, 0, k)),
            ],
        ),
        out_shape=[
            jax.ShapeDtypeStruct(query.shape, jnp.bfloat16),
            jax.ShapeDtypeStruct(query.shape, jnp.bfloat16),
            jax.ShapeDtypeStruct((samples, img_rows, kv.shape[2]), jnp.bfloat16),
        ],
        compiler_params=pltpu.CompilerParams(vmem_limit_bytes=40 * 1024 * 1024),
        cost_estimate=pl.CostEstimate(
            flops=flops, bytes_accessed=8 * query.size, transcendentals=samples * text * cols
        ),
    )(source, count, query, cot, kv, gain.reshape(head_dim, 1), ratio.reshape(1))


def gather_features(image):
    bits = (lax.axis_size("tensor") - 1).bit_length()
    blocks = {0: [image[slot] for slot in range(image.shape[0])]}
    for bit in reversed(range(bits)):
        arrived = {}
        for offset, parts in blocks.items():
            arrived[offset ^ 1 << bit] = [swapped(part, "tensor", bit) for part in parts]
        blocks.update(arrived)
    return blocks


def per_device(
    query,
    image,
    tiles,
    image_slot,
    key_weight_matrix,
    value_weight_matrix,
    query_gain,
    key_gain,
    gate,
    cotangent,
):
    head_dim = query_gain.shape[0]
    samp_local = query.shape[0]
    own_rows, kv_cols = key_weight_matrix.shape
    kv_local = kv_cols // head_dim
    img_rows = image.shape[1]
    image_cols = image.shape[2]
    ratio = jnp.tanh(gate[0])
    top_bit = (lax.axis_size("dp") // 2).bit_length() - 1
    rank = lax.axis_index("dp")
    place = lax.axis_index("tensor")
    first = rank * samp_local
    local_ids = first + jnp.arange(samp_local, dtype=jnp.int32)
    every = jnp.arange(tiles.shape[0], dtype=jnp.int32)
    match = image_slot[None, :] == local_ids[:, None]
    slot_sample = jnp.sum(jnp.where(match, every[None, :], 0), axis=1)
    home_tiles = lax.dynamic_slice_in_dim(tiles, first, samp_local)
    home_slot = lax.dynamic_slice_in_dim(image_slot, first, samp_local)
    slot_away = slot_sample // samp_local != rank
    home_away = home_slot // samp_local != rank
    source = jnp.where(home_away, samp_local, home_slot % samp_local)

    w_own = jnp.stack(
        [
            key_weight_matrix.reshape(own_rows, kv_local, head_dim),
            value_weight_matrix.reshape(own_rows, kv_local, head_dim),
        ],
        axis=2,
    ).reshape(own_rows, 2 * kv_cols)
    w_both = lax.all_gather(w_own, "dp", axis=0, tiled=True)
    width = w_both.shape[0]
    blocks = gather_features(image)
    projected = []
    for slot in range(samp_local):
        total = None
        for offset, parts in blocks.items():
            begin = (place ^ offset) * image_cols
            w_rows = lax.dynamic_slice_in_dim(w_both, begin, image_cols, 0)
            term = jnp.dot(parts[slot], w_rows, preferred_element_type=jnp.float32)
            total = term if total is None else total + term
        projected.append(total)
    projected = jnp.stack(projected).reshape(samp_local, img_rows, kv_local, 2, head_dim)
    kraw = projected[..., 0, :]
    key_factor = rms_factor(kraw)
    keys = kraw * key_factor * key_gain
    kv = jnp.stack([keys, projected[..., 1, :]], axis=3).astype(jnp.bfloat16)
    kv = kv.reshape(samp_local, img_rows, 2 * kv_cols)
    far_kv = swapped(
        lax.dynamic_index_in_dim(kv, jnp.argmax(slot_away), 0, keepdims=True), "dp", top_bit
    )
    context, d_query, home_dkv = attend(
        query,
        cotangent,
        jnp.concatenate([kv, far_kv], axis=0),
        source.astype(jnp.int32),
        home_tiles,
        query_gain,
        ratio,
        kv_local,
        head_dim,
    )
    far_dkv = swapped(
        lax.dynamic_index_in_dim(home_dkv, jnp.argmax(home_away), 0, keepdims=False), "dp", top_bit
    )
    slot_dkv = []
    for slot in range(samp_local):
        near = lax.dynamic_index_in_dim(home_dkv, slot_sample[slot] % samp_local, 0, keepdims=False)
        slot_dkv.append(jnp.where(slot_away[slot], far_dkv, near))
    slot_dkv = jnp.stack(slot_dkv).astype(jnp.float32)
    slot_dkv = slot_dkv.reshape(samp_local, img_rows, kv_local, 2, head_dim)
    d_kraw = norm_back(kraw, key_factor, key_gain, slot_dkv[..., 0, :])
    d_both = jnp.stack([d_kraw, slot_dkv[..., 1, :]], axis=3).astype(jnp.bfloat16)
    d_both = d_both.reshape(samp_local, img_rows, 2 * kv_cols)
    dims = (((0,), (0,)), ((), ()))
    grads = jnp.zeros((width, 2 * kv_cols), jnp.bfloat16)
    for offset, parts in blocks.items():
        total = None
        for slot in range(samp_local):
            term = lax.dot_general(
                parts[slot], d_both[slot], dims, preferred_element_type=jnp.float32
            )
            total = term if total is None else total + term
        grads = lax.dynamic_update_slice_in_dim(
            grads, total.astype(jnp.bfloat16), (place ^ offset) * image_cols, 0
        )
    shares = lax.psum_scatter(grads, "dp", scatter_dimension=0, tiled=True).astype(jnp.float32)
    shares = shares.reshape(own_rows, kv_local, 2, head_dim)
    return (
        context,
        d_query,
        shares[:, :, 0].reshape(own_rows, kv_cols),
        shares[:, :, 1].reshape(own_rows, kv_cols),
    )


def solution(mesh):
    placed = (
        P("dp", None, "tensor"),
        P("dp", None, "tensor"),
        P(),
        P(),
        P("dp", "tensor"),
        P("dp", "tensor"),
        P(),
        P(),
        P(),
        P("dp", None, "tensor"),
    )
    return jax.shard_map(
        per_device,
        mesh=mesh,
        in_specs=placed,
        out_specs=(
            P("dp", None, "tensor"),
            P("dp", None, "tensor"),
            P("dp", "tensor"),
            P("dp", "tensor"),
        ),
        check_vma=False,
    )
```

```python
import functools

import jax
import jax.numpy as jnp
from jax import lax
from jax.experimental import pallas as pl
from jax.experimental.pallas import tpu as pltpu
from jax.sharding import PartitionSpec as P

TILE = 128


EPS = 1e-06


def swapped(shard, axis, distance):
    return lax.ppermute(shard, axis, [(i, i ^ 1 << distance) for i in range(lax.axis_size(axis))])


def rms_factor(values):
    return lax.rsqrt(jnp.mean(values * values, axis=-1, keepdims=True) + EPS)


def norm_back(values, norm_multiplier, gain, grad):
    weighted = grad * gain
    inner = jnp.sum(weighted * values, axis=-1, keepdims=True)
    return (
        norm_multiplier * weighted
        - values * (norm_multiplier * norm_multiplier * norm_multiplier) * inner / values.shape[-1]
    )


def attend_kernel(
    group, source, count, q_ref, cot_ref, kv_ref, gain_ref, ratio_ref, ctx_ref, dq_ref, dkv_ref
):
    own = pl.program_id(0)
    rows = kv_ref.shape[1]
    dim = kv_ref.shape[2] // 2
    text = q_ref.shape[1]
    scale = dim ** (-0.5)
    f32 = jnp.float32
    bf16 = jnp.bfloat16
    tiles = count[own]
    ratio = ratio_ref[0]
    empty = (tiles == 0).astype(f32)
    gain = gain_ref[...]
    keys = kv_ref[0, :, :dim]
    vals = kv_ref[0, :, dim:]
    keys_t = keys.T
    vals_t = vals.T
    at_once = 2 if group % 2 == 0 else 1
    valid = lax.broadcasted_iota(jnp.int32, (rows, at_once * text), 0) < tiles * TILE
    across = (((1,), (1,)), ((), ()))
    d_keys = jnp.zeros((rows, dim), f32)
    d_vals = jnp.zeros((rows, dim), f32)

    def load(ref, first):
        parts = [
            ref[0, :, (first + i) * dim : (first + i + 1) * dim].astype(f32).T
            for i in range(at_once)
        ]
        return jnp.concatenate(parts, axis=1)

    def store(ref, first, value):
        for i in range(at_once):
            part = value[:, i * text : (i + 1) * text].T
            ref[0, :, (first + i) * dim : (first + i + 1) * dim] = part.astype(bf16)

    for first in range(0, group, at_once):
        q_raw = load(q_ref, first)
        d_att = ratio * load(cot_ref, first)
        q_factor = lax.rsqrt(jnp.mean(q_raw * q_raw, axis=0, keepdims=True) + EPS)
        q_norm = (q_raw * q_factor * gain).astype(bf16)
        scores = jnp.dot(keys, q_norm, preferred_element_type=f32) * scale
        expo = jnp.where(valid, jnp.exp(scores), 0.0)
        total = jnp.sum(expo, axis=0, keepdims=True) + empty
        inverse = 1.0 / total
        weights_b = expo.astype(bf16)
        attended = jnp.dot(vals_t, weights_b, preferred_element_type=f32) * inverse
        store(ctx_ref, first, ratio * attended)
        d_att_b = d_att.astype(bf16)
        scaled_b = (d_att * inverse).astype(bf16)
        delta = jnp.sum(d_att * attended, axis=0, keepdims=True)
        d_prob = jnp.dot(vals, d_att_b, preferred_element_type=f32)
        d_score = (expo * inverse * (d_prob - delta)).astype(bf16)
        d_qn = scale * jnp.dot(keys_t, d_score, preferred_element_type=f32)
        weighted = d_qn * gain
        inner = jnp.sum(weighted * q_raw, axis=0, keepdims=True)
        cubed = q_factor * q_factor * q_factor
        store(dq_ref, first, q_factor * weighted - q_raw * (cubed * inner / dim))
        d_keys += lax.dot_general(d_score, q_norm, across, preferred_element_type=f32)
        d_vals += lax.dot_general(weights_b, scaled_b, across, preferred_element_type=f32)
    dkv_ref[0, :, :dim] = (scale * d_keys).astype(bf16)
    dkv_ref[0, :, dim:] = d_vals.astype(bf16)


def attend(query, cot, kv, source, count, gain, ratio, head, kv_local):
    samples, text, cols = query.shape
    img_rows = kv.shape[1]
    head_dim = gain.shape[0]
    head_cols = cols // kv_local
    group = head_cols // head_dim
    per_head = pl.BlockSpec((1, text, head_cols), lambda s, *_: (s, 0, head))
    alone = pl.BlockSpec((1, text, head_cols), lambda s, *_: (s, 0, 0))
    out = jax.ShapeDtypeStruct((samples, text, head_cols), jnp.bfloat16)
    return pl.pallas_call(
        functools.partial(attend_kernel, group),
        grid_spec=pltpu.PrefetchScalarGridSpec(
            num_scalar_prefetch=2,
            grid=(samples,),
            in_specs=[
                per_head,
                per_head,
                pl.BlockSpec(
                    (1, img_rows, 2 * head_dim), lambda s, source, count: (source[s], 0, 0)
                ),
                pl.BlockSpec((head_dim, 1), lambda s, *_: (0, 0)),
                pl.BlockSpec(memory_space=pltpu.SMEM),
            ],
            out_specs=[
                alone,
                alone,
                pl.BlockSpec((1, img_rows, 2 * head_dim), lambda s, *_: (s, 0, 0)),
            ],
        ),
        out_shape=[
            out,
            out,
            jax.ShapeDtypeStruct((samples, img_rows, 2 * head_dim), jnp.bfloat16),
        ],
        compiler_params=pltpu.CompilerParams(vmem_limit_bytes=32 * 1024 * 1024),
        cost_estimate=pl.CostEstimate(
            flops=12 * samples * text * head_cols * img_rows,
            bytes_accessed=8 * samples * text * head_cols,
            transcendentals=samples * text * group * img_rows,
        ),
    )(source, count, query, cot, kv, gain.reshape(head_dim, 1), ratio.reshape(1))


def gather_features(image):
    bits = (lax.axis_size("tensor") - 1).bit_length()
    blocks = {0: [image[slot] for slot in range(image.shape[0])]}
    for bit in reversed(range(bits)):
        arrived = {}
        for offset, parts in blocks.items():
            arrived[offset ^ 1 << bit] = [swapped(part, "tensor", bit) for part in parts]
        blocks.update(arrived)
    return blocks


def per_device(
    query,
    image,
    tiles,
    image_slot,
    key_weight_matrix,
    value_weight_matrix,
    query_gain,
    key_gain,
    gate,
    cotangent,
):
    head_dim = query_gain.shape[0]
    samp_local = query.shape[0]
    own_rows, kv_cols = key_weight_matrix.shape
    kv_local = kv_cols // head_dim
    img_rows = image.shape[1]
    image_cols = image.shape[2]
    ratio = jnp.tanh(gate[0])
    top_bit = (lax.axis_size("dp") // 2).bit_length() - 1
    rank = lax.axis_index("dp")
    place = lax.axis_index("tensor")
    first = rank * samp_local
    local_ids = first + jnp.arange(samp_local, dtype=jnp.int32)
    every = jnp.arange(tiles.shape[0], dtype=jnp.int32)
    match = image_slot[None, :] == local_ids[:, None]
    slot_sample = jnp.sum(jnp.where(match, every[None, :], 0), axis=1)
    home_tiles = lax.dynamic_slice_in_dim(tiles, first, samp_local)
    home_slot = lax.dynamic_slice_in_dim(image_slot, first, samp_local)
    slot_away = slot_sample // samp_local != rank
    home_away = home_slot // samp_local != rank
    source = jnp.where(home_away, samp_local, home_slot % samp_local)

    source = source.astype(jnp.int32)
    slot_sent = jnp.argmax(slot_away)
    home_sent = jnp.argmax(home_away)

    heads = range(kv_local)
    w_heads = []
    for head in heads:
        cols = slice(head * head_dim, (head + 1) * head_dim)
        w_own = jnp.concatenate([key_weight_matrix[:, cols], value_weight_matrix[:, cols]], axis=1)
        w_heads.append(lax.all_gather(w_own, "dp", axis=0, tiled=True))
    width = w_heads[0].shape[0]
    blocks = gather_features(image)

    def project(head):
        projected = []
        for slot in range(samp_local):
            total = None
            for offset, parts in blocks.items():
                begin = (place ^ offset) * image_cols
                w_rows = lax.dynamic_slice_in_dim(w_heads[head], begin, image_cols, 0)
                term = jnp.dot(parts[slot], w_rows, preferred_element_type=jnp.float32)
                total = term if total is None else total + term
            projected.append(total)
        projected = jnp.stack(projected)
        kraw = projected[..., :head_dim]
        key_factor = rms_factor(kraw)
        keys = kraw * key_factor * key_gain
        kv = jnp.concatenate([keys, projected[..., head_dim:]], axis=2).astype(jnp.bfloat16)
        sent = lax.dynamic_index_in_dim(kv, slot_sent, 0, keepdims=True)
        return kraw, key_factor, kv, swapped(sent, "dp", top_bit)

    def weight_share(head, kraw, key_factor, home_dkv):
        sent = lax.dynamic_index_in_dim(home_dkv, home_sent, 0, keepdims=False)
        far_dkv = swapped(sent, "dp", top_bit)
        slot_dkv = []
        for slot in range(samp_local):
            index = slot_sample[slot] % samp_local
            near = lax.dynamic_index_in_dim(home_dkv, index, 0, keepdims=False)
            slot_dkv.append(jnp.where(slot_away[slot], far_dkv, near))
        slot_dkv = jnp.stack(slot_dkv).astype(jnp.float32)
        d_kraw = norm_back(kraw, key_factor, key_gain, slot_dkv[..., :head_dim])
        d_both = jnp.concatenate([d_kraw, slot_dkv[..., head_dim:]], axis=2).astype(jnp.bfloat16)
        dims = (((0,), (0,)), ((), ()))
        grads = jnp.zeros((width, 2 * head_dim), jnp.bfloat16)
        for offset, parts in blocks.items():
            total = None
            for slot in range(samp_local):
                term = lax.dot_general(
                    parts[slot], d_both[slot], dims, preferred_element_type=jnp.float32
                )
                total = term if total is None else total + term
            grads = lax.dynamic_update_slice_in_dim(
                grads, total.astype(jnp.bfloat16), (place ^ offset) * image_cols, 0
            )
        return grads

    context, d_query, shares = [], [], []
    before = None
    for head in heads:
        if before is not None:
            w_heads[head], home_dkv = lax.optimization_barrier((w_heads[head], before[2]))
            before = (before[0], before[1], home_dkv)
        kraw, key_factor, kv, far_kv = project(head)
        q_in = query
        if before is not None:
            grads, q_in = lax.optimization_barrier((weight_share(head - 1, *before), query))
            shares.append(lax.psum_scatter(grads, "dp", scatter_dimension=0, tiled=True))
        ctx, d_q, home_dkv = attend(
            q_in,
            cotangent,
            jnp.concatenate([kv, far_kv], axis=0),
            source,
            home_tiles,
            query_gain,
            ratio,
            head,
            kv_local,
        )
        context.append(ctx)
        d_query.append(d_q)
        before = (kraw, key_factor, home_dkv)
    grads = weight_share(kv_local - 1, *before)
    shares.append(lax.psum_scatter(grads, "dp", scatter_dimension=0, tiled=True))
    shares = [share.astype(jnp.float32) for share in shares]
    return (
        jnp.concatenate(context, axis=2),
        jnp.concatenate(d_query, axis=2),
        jnp.concatenate([share[:, :head_dim] for share in shares], axis=1),
        jnp.concatenate([share[:, head_dim:] for share in shares], axis=1),
    )


def solution(mesh):
    placed = (
        P("dp", None, "tensor"),
        P("dp", None, "tensor"),
        P(),
        P(),
        P("dp", "tensor"),
        P("dp", "tensor"),
        P(),
        P(),
        P(),
        P("dp", None, "tensor"),
    )
    return jax.shard_map(
        per_device,
        mesh=mesh,
        in_specs=placed,
        out_specs=(
            P("dp", None, "tensor"),
            P("dp", None, "tensor"),
            P("dp", "tensor"),
            P("dp", "tensor"),
        ),
        check_vma=False,
    )
```
